512 devices in a mesh: chaos: 64 (over y, x, z_hi, core), space: 8 (over z_lo).
Axes of the slice: x: 4, y: 4, z: 16 (z_hi: 2, z_lo: 8; z = z_hi * 8 + z_lo), core: 2. Of those that a mesh axis runs over, the one named last changes fastest.
Arguments:
- panels: bfloat16 [256, 131072], P('chaos', 'space'), may hold values from -6 to 6
- tiles: bfloat16 [20, 8, 128, 3, 128, 128], P(None, 'space', 'chaos'), may hold values from -0.3125 to 0.3125
- coupling: bfloat16 [256, 20, 256], P('chaos'), may hold values from -0.125 to 0.125
- pattern: int32 [20, 4, 4], replicated, may hold values 0 or 1
- colidx: int32 [8, 128, 3], P('space', 'chaos'), may hold values from -2 to 1025, as said below
Outputs:
- applied: bfloat16 [256, 131072], P('chaos', 'space')
The draws below stay inside these ranges and needn't reach their ends.
Inputs may be any that keep to these rules, and one draw needn't show every extreme that they name: `colidx`: row block r names 3 distinct tile columns: r itself and 2 of r - 2, r - 1, r + 1, r + 2; columns outside 0 .. 1023 stand for blocks of zeros.
All inputs are finite; a program needn't handle non-finite values.
Results may differ from the reference program's by a relative error of at most 0.005.
Values may be sent and summed in bfloat16 or wider, within the bound.
A program may use at most 64 MiB of HBM per device.

```python
import jax
import jax.numpy as jnp
from jax import lax

M = 20
TILE = 128
NNZ = 3
CBLK = 64
RB_DEV = 128
P_SIZE = 256
PB = 4
SLABS = 8
RBTOT = 1024
NS = 131072


def draw_colidx(key, part):
    key = jax.random.fold_in(key, 11)
    scores = jax.random.randint(key, (SLABS, RB_DEV, 4), 0, 1 << 20) * 4 + jnp.arange(4, dtype=jnp.int32)
    row_ids = jnp.arange(SLABS * RB_DEV, dtype=jnp.int32).reshape(SLABS, RB_DEV)
    slot_ids = jnp.arange(4, dtype=jnp.int32)
    at_first = (row_ids == 0)[..., None] & (slot_ids == 0)
    at_last = (row_ids == SLABS * RB_DEV - 1)[..., None] & (slot_ids == 3)
    scores = jnp.where(at_first | at_last, -1, scores)
    order = jnp.argsort(scores, axis=-1)
    offsets = jnp.array([-2, -1, 1, 2], jnp.int32)
    picked = offsets[order[..., :NNZ - 1]]
    diagonal = jnp.zeros((SLABS, RB_DEV, 1), jnp.int32)
    return (jnp.concatenate([diagonal, picked], axis=-1) + row_ids[..., None]).astype(jnp.int32)


def place_ends(result, stream_key, low, top_value):
    index_at = [jax.random.randint(jax.random.fold_in(stream_key, axis), (), 0, length) for axis, length in enumerate(result.shape)]
    longest = result.shape.index(max(result.shape))
    beside = index_at[:longest] + [(index_at[longest] + 1) % result.shape[longest]] + index_at[longest + 1:]
    return result.at[tuple(index_at)].set(low).at[tuple(beside)].set(top_value)


def steps_of(own_key, shape, shards, smallest, top_value):
    gain = 1.0
    for axis_at, parts in shards:
        draws = jax.random.uniform(jax.random.fold_in(jax.random.fold_in(own_key, 6), axis_at), (parts,), jnp.float32, smallest / len(shards), top_value / len(shards))
        gain = gain * jnp.repeat(jnp.exp(draws), shape[axis_at] // parts).reshape((-1,) + (1,) * (len(shape) - 1 - axis_at))
    return gain


def centred(rng, dims, width, bound, shards=(), held_as=jnp.bfloat16):
    drawn = width * jax.random.normal(rng, dims, jnp.float32)
    if shards:
        drawn = drawn * steps_of(rng, dims, shards, -0.22, 0.18)
    return jnp.clip(drawn, -bound, bound).astype(held_as)


def setup_inputs(seed: int = 0) -> dict:
    key_list = jax.random.split(jax.random.key(seed), 6)
    return {
        "panels": centred(key_list[0], (P_SIZE, NS), 1.0, 6.0, ((0, 64), (1, 8))),
        "tiles": centred(key_list[1], (M, SLABS, RB_DEV, NNZ, TILE, TILE), (NNZ * TILE) ** -0.5, 0.3125, ((1, 8), (2, 64))),
        "coupling": centred(key_list[2], (P_SIZE, M, P_SIZE), (M * P_SIZE // 2) ** -0.5, 0.125, ((0, 64),)),
        "pattern": place_ends((jax.random.randint(key_list[3], (M, PB, PB), 0, 2) < 1).astype(jnp.int32), jax.random.fold_in(key_list[3], 1), 0, 1),
        "colidx": draw_colidx(jax.random.fold_in(key_list[5], 71), 0),
    }


def reference(panels, tiles, coupling, pattern, colidx):
    masks = jnp.repeat(jnp.repeat(pattern, CBLK, axis=1), CBLK, axis=2)
    effective = coupling * jnp.transpose(masks, (1, 0, 2)).astype(jnp.bfloat16)
    eff_wide = effective.astype(jnp.float32)
    blocks_all = panels.reshape(P_SIZE, RBTOT, TILE)
    zero_pad = jnp.zeros((P_SIZE, 2, TILE), panels.dtype)
    padded = jnp.concatenate([zero_pad, blocks_all, zero_pad], axis=1)
    flat_tiles = tiles.reshape(M, RBTOT, NNZ, TILE, TILE)
    flat_cols = colidx.reshape(RBTOT, NNZ).astype(jnp.int32)

    def block_terms(index):
        tile_row = lax.dynamic_index_in_dim(flat_tiles, index, 1, keepdims=False)
        columns = lax.dynamic_index_in_dim(flat_cols, index, 0, keepdims=False) + 2
        picked = jnp.take(padded, columns, axis=1).astype(jnp.float32)
        projected = jnp.einsum('mqtc,aqc->mta', tile_row.astype(jnp.float32), picked)
        projected = projected.astype(jnp.bfloat16).astype(jnp.float32)
        return jnp.einsum('mta,amb->bt', projected, eff_wide)

    outputs = lax.map(block_terms, jnp.arange(RBTOT, dtype=jnp.int32))
    return jnp.transpose(outputs, (1, 0, 2)).reshape(P_SIZE, NS).astype(jnp.bfloat16)
```

```python
import jax
import jax.numpy as jnp
from jax import lax
from jax.experimental import pallas as pl
from jax.experimental.pallas import tpu as pltpu
from jax.sharding import PartitionSpec as P

M = 20
TILE = 128
CBLK = 64
BF = jnp.bfloat16
F32 = jnp.float32
UNITS = 33
SPLIT = 48
ORDER = (2, 1, 3, 0)


def perm(rows, source_of):
    out_row = lax.broadcasted_iota(jnp.int32, (rows, rows), 0)
    in_row = lax.broadcasted_iota(jnp.int32, (rows, rows), 1)
    return jnp.where(in_row == source_of(out_row), 1.0, 0.0).astype(BF)


def matmul(a, b):
    return lax.dot_general(a, b, (((1,), (0,)), ((), ())), preferred_element_type=F32)


def matmul_nt(a, b):
    return lax.dot_general(a, b, (((1,), (1,)), ((), ())), preferred_element_type=F32)


def kernel(cols, u, chunk, tiles, out,
           tv, uin, ufix, vbuf, xraw, xw, eraw, ew, zbuf, acc, ob, oin, fb,
           s_t, s_v, r_v, s_e, r_e, s_u, r_u, s_a, r_a, s_b, r_b, s_d, r_d, s_x, r_x, s_o, r_o, s_p, r_p):
    rank = lax.axis_index("chaos")
    s = lax.axis_index("space")
    c = rank % 2
    h = (rank // 2) % 2
    yx = rank // 4
    y = yx // 4
    x = yx % 4

    def remote(src, dst, send, recv, chaos, space=None):
        return pltpu.make_async_remote_copy(
            src_ref=src, dst_ref=dst, send_sem=send, recv_sem=recv,
            device_id={"chaos": chaos, "space": s if space is None else space},
            device_id_type=pl.DeviceIdType.MESH)

    def wait_for(ref, sem):
        pltpu.make_async_copy(ref, ref, sem).wait()

    def in_plane(dest_yx, dest_c):
        return (dest_yx * 2 + h) * 2 + dest_c

    anti = (yx * 2 + 1 - h) * 2 + c
    mate = (yx * 2 + h) * 2 + 1 - c
    low, high = s > 0, s < 7
    flat = yx * 4 + c

    load = pltpu.make_async_copy(tiles, tv, s_t)
    load.start()

    barrier = pltpu.get_barrier_semaphore()

    def greet(chaos, space):
        pl.semaphore_signal(barrier, inc=1, device_id={"chaos": chaos, "space": space},
                            device_id_type=pl.DeviceIdType.MESH)

    greet(anti, s)

    @pl.when(high)
    def _():
        greet(flat + 2 * h, s + 1)

    @pl.when(low)
    def _():
        greet(flat + 2 * h, s - 1)

    @pl.when(low & (h == 0))
    def _():
        greet(flat + 2, s - 1)

    @pl.when(high & (h == 1))
    def _():
        greet(flat, s + 1)

    def greet_plane(d, carry):
        other = (yx * 2 + c + d) % 32
        greet(in_plane(other // 2, other % 2), s)
        return carry

    lax.fori_loop(1, 32, greet_plane, 0)
    has_halo = (low & (h == 0)) | (high & (h == 1))
    pl.semaphore_wait(barrier, 32 + low.astype(jnp.int32) + high.astype(jnp.int32) + has_halo.astype(jnp.int32))

    send_right = remote(u.at[UNITS - 1], vbuf.at[h], s_v.at[0], r_v.at[h], flat, jnp.minimum(s + 1, 7))
    send_left = remote(u.at[0], vbuf.at[1 - h], s_v.at[1], r_v.at[1 - h], flat + 2, jnp.maximum(s - 1, 0))

    @pl.when(high)
    def _():
        send_right.start()

    @pl.when(low)
    def _():
        send_left.start()

    cross_e = remote(chunk, eraw.at[c, 1, y, x], s_e, r_e, anti)
    cross_e.start()
    crossings = []
    for i, shift in enumerate(ORDER):
        start = ((y + shift) % 4) * 8 + 1 - h
        crossing = remote(u.at[pl.ds(start, 8)], uin.at[pl.ds(start, 8)], s_u.at[i], r_u.at[i], anti)
        crossing.start()
        crossings.append(crossing)

    first = pl.ds(0, SPLIT)
    second = pl.ds(SPLIT, 80 - SPLIT)

    def phase_a(src, half):
        mine = eraw.at[c, half, y, x]
        for d in (1, 2, 3):
            remote(src.at[first], mine.at[first], s_a.at[half, 0], r_a.at[half, 0],
                   in_plane(y * 4 + (x + d) % 4, c)).start()
            remote(src.at[second], mine.at[second], s_a.at[half, 1], r_a.at[half, 1],
                   in_plane(((y + d) % 4) * 4 + x, c)).start()

    def phase_b(half):
        part = eraw.at[c, half]
        wait_for(part.at[0, pl.ds(0, 3), first], r_a.at[half, 0])
        row = part.at[y, :, first]
        for d in (1, 2, 3):
            remote(row, row, s_b.at[half, 0], r_b.at[half, 0], in_plane(((y + d) % 4) * 4 + x, c)).start()
        wait_for(part.at[0, pl.ds(0, 3), second], r_a.at[half, 1])
        column = part.at[:, x, second]
        for d in (1, 2, 3):
            remote(column, column, s_b.at[half, 1], r_b.at[half, 1], in_plane(y * 4 + (x + d) % 4, c)).start()

    def phase_d(half):
        part = eraw.at[c, half]
        wait_for(part.at[pl.ds(0, 3), :, first], r_b.at[half, 0])
        wait_for(part.at[pl.ds(0, 3), :, second], r_b.at[half, 1])
        remote(part, part, s_d.at[half], r_d.at[half], mate).start()

    def finish_e(half):
        part = eraw.at[c, half]
        wait_for(part.at[0, pl.ds(0, 3), first], s_a.at[half, 0])
        wait_for(part.at[0, pl.ds(0, 3), second], s_a.at[half, 1])
        wait_for(part.at[pl.ds(0, 3), :, first], s_b.at[half, 0])
        wait_for(part.at[pl.ds(0, 3), :, second], s_b.at[half, 1])
        wait_for(part, s_d.at[half])

    phase_a(chunk, 0)
    eraw[c, 0, y, x] = chunk[...]

    hub = 15 * h
    slot = yx * 2 + c

    def serve_row(src, half, shift):
        dest_y = (y + shift) % 4

        def serve(i, carry):
            dest = dest_y * 4 + (x + i // 2) % 4
            dest_c = (c + i % 2) % 2

            @pl.when((dest != hub) & (dest * 2 + dest_c != slot))
            def _():
                remote(src.at[pl.ds(dest * 2 + h, 2)], xraw.at[half, slot], s_x.at[half], r_x.at[half],
                       in_plane(dest, dest_c)).start()

            return carry

        lax.fori_loop(0, 8, serve, 0)

    def serve_hub(src, half):
        @pl.when(has_halo)
        def _():
            wait_for(vbuf.at[half], r_v.at[half])

        @pl.when(jnp.logical_not(has_halo))
        def _():
            vbuf[half] = jnp.zeros((16, TILE), BF)

        halo = vbuf[half]
        none = jnp.zeros_like(halo)
        ufix[half, 0] = src[31 * h] + jnp.where(h == 0, halo, none)
        ufix[half, 1] = src[31 * h + 1] + jnp.where(h == 1, halo, none)
        for dest_c in (0, 1):
            @pl.when(hub * 2 + dest_c != slot)
            def _():
                remote(ufix.at[half], xraw.at[half, slot], s_x.at[half], r_x.at[half],
                       in_plane(hub, dest_c)).start()

        @pl.when(yx == hub)
        def _():
            xraw[half, slot] = ufix[half]

        @pl.when(yx != hub)
        def _():
            xraw[half, slot] = src[pl.ds(yx * 2 + h, 2)]

    for shift in ORDER:
        serve_row(u, 0, shift)
    phase_b(0)
    serve_hub(u, 0)

    cross_e.wait_recv()
    phase_a(eraw.at[c, 1, y, x], 1)
    phase_d(0)
    for i, shift in enumerate(ORDER):
        crossings[i].wait_recv()
        serve_row(uin, 1, shift)
        if i == 1:
            phase_b(1)
    serve_hub(uin, 1)

    x_perm = perm(256, lambda o: ((o % 32) // 4) * 32 + (o // 32) * 4 + o % 4)
    e_perm = perm(256, lambda o: ((o % 8) // 4) * 128 + ((o % 64) // 8) * 16 + (o // 64) * 4 + o % 4)

    def ready_x(half):
        wait_for(xraw.at[half, pl.ds(0, 31)], r_x.at[half])
        for g in range(4):
            part = matmul(x_perm, xraw[half, pl.ds(g * 8, 8)].reshape(256, TILE)).astype(BF)
            for block in range(8):
                xw[half, block, pl.ds(g * 32, 32)] = part[block * 32:(block + 1) * 32]

    def ready_e(half):
        wait_for(eraw.at[1 - c, half], r_d.at[half])

        def group(kg, carry):
            rows = pl.ds(pl.multiple_of(kg * 16, 16), 16)
            for g in range(2):
                raw = eraw[:, half, pl.ds(g * 2, 2), :, rows]
                part = matmul(e_perm, raw.reshape(256, 256)).astype(BF)
                for k in range(4):
                    ew[half, kg * 4 + k, pl.ds(g * 64, 64)] = part[k * 64:(k + 1) * 64]
            return carry

        lax.fori_loop(0, 5, group, 0)

    def stage_one(half):
        for r in range(2):
            picked = [xw[half, cols[r, q]] for q in range(3)]
            pair = jnp.concatenate(picked[:2], axis=1)

            def some(kg, carry):
                part = tv[pl.ds(kg * 4, 4), r]
                left = jnp.concatenate([part[:, 0], part[:, 1]], axis=2).reshape(512, 256)
                z = matmul_nt(left, pair) + matmul_nt(part[:, 2].reshape(512, TILE), picked[2])
                z = z.astype(BF)
                for k in range(4):
                    zbuf[kg * 2 + k // 2, pl.ds(r * TILE, TILE), pl.ds((k % 2) * TILE, TILE)] = z[k * TILE:(k + 1) * TILE]
                return carry

            lax.fori_loop(0, 5, some, 0)

    def stage_two(half):
        def pair_of(kk, total):
            return total + matmul(zbuf[kk], ew[half, pl.ds(kk * 2, 2)].reshape(256, 256))

        return lax.fori_loop(0, 10, pair_of, jnp.zeros((256, 256), F32))

    load.wait()
    ready_x(0)
    stage_one(0)
    phase_d(1)
    ready_e(0)
    acc[...] = stage_two(0)
    ready_e(1)
    ready_x(1)
    stage_one(1)
    total = (acc[...] + stage_two(1)).astype(BF)

    o_perm = perm(256, lambda o: ((o % 64) // 4) * 16 + (o // 128) * 8 + ((o % 128) // 64) * 4 + o % 4)
    ob[...] = matmul_nt(o_perm, total).astype(BF)
    cross_o = remote(ob.at[pl.ds(pl.multiple_of((1 - h) * 128, 128), 128)], oin, s_o, r_o, anti)
    cross_o.start()
    mine = ob[pl.ds(pl.multiple_of(h * 128, 128), 128)]
    f_perm = perm(256, lambda o: ((o % 16) // 4) * 64 + (o // 16) * 4 + o % 4)
    cross_o.wait_recv()
    theirs = oin[...]
    lower = jnp.where(h == 0, mine, theirs)
    upper = jnp.where(h == 0, theirs, mine)
    for dest_c in range(2):
        rows = slice(dest_c * 64, dest_c * 64 + 64)
        stack = jnp.concatenate([lower[rows, :TILE], lower[rows, TILE:], upper[rows, :TILE], upper[rows, TILE:]], axis=0)
        fb[dest_c] = matmul(f_perm, stack).astype(BF).reshape(16, 16, TILE)

    def give(d, carry):
        other = (slot + d) % 32
        remote(fb.at[other % 2, other // 2], out.at[slot], s_p, r_p, in_plane(other // 2, other % 2)).start()
        return carry

    lax.fori_loop(1, 32, give, 0)
    out[slot] = fb[c, yx]

    @pl.when(high)
    def _():
        send_right.wait_send()

    @pl.when(low)
    def _():
        send_left.wait_send()

    cross_e.wait_send()
    for crossing in crossings:
        crossing.wait_send()
    for half in (0, 1):
        finish_e(half)
        wait_for(xraw.at[half, pl.ds(0, 31)], s_x.at[half])
    cross_o.wait_send()
    wait_for(out.at[pl.ds(0, 31)], s_p)
    wait_for(out.at[pl.ds(0, 31)], r_p)


def shards(panels, tiles, coupling, pattern, colidx):
    rank = lax.axis_index("chaos")
    space = lax.axis_index("space")
    cells = jnp.transpose(panels.reshape(4, 128, TILE), (1, 0, 2)).reshape(512, TILE)
    units = jnp.pad(cells, ((8, 8), (0, 0))).reshape(UNITS, 16, TILE)
    own_pattern = lax.dynamic_index_in_dim(pattern, rank // 16, 1, keepdims=False).astype(BF)
    mask = jnp.broadcast_to(own_pattern[:, None, :, None], (M, 4, 4, CBLK)).reshape(M, 4, 256)
    chunk = (jnp.transpose(coupling, (1, 0, 2)) * mask).reshape(80, 256)
    cols = colidx[0] - (space * 128 + (rank // 2) * 4) + 2
    vmem = pl.BlockSpec(memory_space=pltpu.VMEM)
    dma = pltpu.SemaphoreType.DMA
    result = pl.pallas_call(
        kernel,
        name="galerkin",
        out_shape=jax.ShapeDtypeStruct((32, 16, TILE), BF),
        in_specs=[pl.BlockSpec(memory_space=pltpu.SMEM), vmem, vmem, pl.BlockSpec(memory_space=pl.ANY)],
        out_specs=vmem,
        scratch_shapes=[
            pltpu.VMEM((M, 2, 3, TILE, TILE), BF),
            pltpu.VMEM((UNITS, 16, TILE), BF),
            pltpu.VMEM((2, 2, 16, TILE), BF),
            pltpu.VMEM((2, 16, TILE), BF),
            pltpu.VMEM((2, 32, 2, 16, TILE), BF),
            pltpu.VMEM((2, 8, TILE, TILE), BF),
            pltpu.VMEM((2, 2, 4, 4, 80, 256), BF),
            pltpu.VMEM((2, M, TILE, 256), BF),
            pltpu.VMEM((10, 256, 256), BF),
            pltpu.VMEM((256, 256), F32),
            pltpu.VMEM((256, 256), BF),
            pltpu.VMEM((TILE, 256), BF),
            pltpu.VMEM((2, 16, 16, TILE), BF),
            dma, dma((2,)), dma((2,)), dma, dma, dma((4,)), dma((4,)),
            dma((2, 2)), dma((2, 2)), dma((2, 2)), dma((2, 2)), dma((2,)), dma((2,)), dma((2,)), dma((2,)),
            dma, dma, dma, dma,
        ],
        compiler_params=pltpu.CompilerParams(collective_id=0, has_side_effects=True, vmem_limit_bytes=40 << 20),
        cost_estimate=pl.CostEstimate(flops=2_000_000_000, bytes_accessed=8_000_000, transcendentals=0),
    )(cols, units, chunk, tiles.reshape(M, 2, 3, TILE, TILE))
    parts = result.reshape(16, 2, 2, 2, 4, TILE)
    return jnp.transpose(parts, (4, 0, 2, 1, 3, 5)).reshape(4, 128 * TILE)


def solution(mesh):
    in_specs = (
        P("chaos", "space"),
        P(None, "space", "chaos", None, None, None),
        P("chaos", None, None),
        P(),
        P("space", "chaos", None),
    )
    return jax.shard_map(shards, mesh=mesh, in_specs=in_specs, out_specs=P("chaos", "space"), check_vma=False)
```

```python
import jax
import jax.numpy as jnp
from jax import lax
from jax.experimental import pallas as pl
from jax.experimental.layout import Layout, with_layout_constraint
from jax.experimental.pallas import tpu as pltpu
from jax.sharding import PartitionSpec as P

M = 20
TILE = 128
CBLK = 64
BF = jnp.bfloat16
F32 = jnp.float32
UNITS = 33
SPLIT = 48
ORDER = (2, 1, 3, 0)


def perm(rows, source_of):
    out_row = lax.broadcasted_iota(jnp.int32, (rows, rows), 0)
    in_row = lax.broadcasted_iota(jnp.int32, (rows, rows), 1)
    return jnp.where(in_row == source_of(out_row), 1.0, 0.0).astype(BF)


def matmul(a, b):
    return lax.dot_general(a, b, (((1,), (0,)), ((), ())), preferred_element_type=F32)


def matmul_nt(a, b):
    return lax.dot_general(a, b, (((1,), (1,)), ((), ())), preferred_element_type=F32)


def kernel(colidx, cells, coupling, pattern, tiles, out,
           u, chunk, tv, uin, ufix, vbuf, xraw, xw, eraw, ew, zbuf, acc, ob, oin, fb,
           s_t, s_v, r_v, s_e, r_e, s_u, r_u, s_a, r_a, s_b, r_b, s_d, r_d, s_x, r_x, s_o, r_o, s_p, r_p):
    rank = lax.axis_index("chaos")
    s = lax.axis_index("space")
    c = rank % 2
    h = (rank // 2) % 2
    yx = rank // 4
    y = yx // 4
    x = yx % 4

    def remote(src, dst, send, recv, chaos, space=None):
        return pltpu.make_async_remote_copy(
            src_ref=src, dst_ref=dst, send_sem=send, recv_sem=recv,
            device_id={"chaos": chaos, "space": s if space is None else space},
            device_id_type=pl.DeviceIdType.MESH)

    def wait_for(ref, sem):
        pltpu.make_async_copy(ref, ref, sem).wait()

    def in_plane(dest_yx, dest_c):
        return (dest_yx * 2 + h) * 2 + dest_c

    anti = (yx * 2 + 1 - h) * 2 + c
    mate = (yx * 2 + h) * 2 + 1 - c
    low, high = s > 0, s < 7
    flat = yx * 4 + c
    first_col = s * 128 + (rank // 2) * 4 - 2

    load = pltpu.make_async_copy(tiles, tv, s_t)
    load.start()

    barrier = pltpu.get_barrier_semaphore()

    def greet(chaos, space):
        pl.semaphore_signal(barrier, inc=1, device_id={"chaos": chaos, "space": space},
                            device_id_type=pl.DeviceIdType.MESH)

    greet(anti, s)

    @pl.when(high)
    def _():
        greet(flat + 2 * h, s + 1)

    @pl.when(low)
    def _():
        greet(flat + 2 * h, s - 1)

    @pl.when(low & (h == 0))
    def _():
        greet(flat + 2, s - 1)

    @pl.when(high & (h == 1))
    def _():
        greet(flat, s + 1)

    def greet_plane(d, carry):
        other = (yx * 2 + c + d) % 32
        greet(in_plane(other // 2, other % 2), s)
        return carry

    lax.fori_loop(1, 32, greet_plane, 0)
    has_halo = (low & (h == 0)) | (high & (h == 1))

    row = lax.broadcasted_iota(jnp.int32, (80, M), 0)
    term = lax.broadcasted_iota(jnp.int32, (80, M), 1)
    spread = jnp.where(row // 4 == term, 1.0, 0.0).astype(BF)
    block = lax.broadcasted_iota(jnp.int32, (4, 256), 0)
    column = lax.broadcasted_iota(jnp.int32, (4, 256), 1)
    widen = jnp.where(column // CBLK == block, 1.0, 0.0).astype(BF)
    mask = matmul(matmul_nt(spread, pattern[y].astype(F32).astype(BF)).astype(BF), widen)
    out_row = lax.broadcasted_iota(jnp.int32, (80, 160), 0)
    in_row = lax.broadcasted_iota(jnp.int32, (80, 160), 1)
    raw = coupling[...].reshape(160, TILE)
    for part in range(2):
        take = jnp.where(in_row == (out_row // 4) * 8 + part * 4 + out_row % 4, 1.0, 0.0).astype(BF)
        lanes = slice(part * TILE, part * TILE + TILE)
        chunk[:, lanes] = (matmul(take, raw) * mask[:, lanes]).astype(BF)

    gap = jnp.zeros((8, TILE), BF)
    u[...] = jnp.concatenate([gap, cells[...].reshape(512, TILE), gap], axis=0).reshape(UNITS, 16, TILE)
    pl.semaphore_wait(barrier, 32 + low.astype(jnp.int32) + high.astype(jnp.int32) + has_halo.astype(jnp.int32))

    send_right = remote(u.at[UNITS - 1], vbuf.at[h], s_v.at[0], r_v.at[h], flat, jnp.minimum(s + 1, 7))
    send_left = remote(u.at[0], vbuf.at[1 - h], s_v.at[1], r_v.at[1 - h], flat + 2, jnp.maximum(s - 1, 0))

    @pl.when(high)
    def _():
        send_right.start()

    @pl.when(low)
    def _():
        send_left.start()

    cross_e = remote(chunk, eraw.at[c, 1, y, x], s_e, r_e, anti)
    cross_e.start()
    crossings = []
    for i, shift in enumerate(ORDER):
        start = ((y + shift) % 4) * 8 + 1 - h
        crossing = remote(u.at[pl.ds(start, 8)], uin.at[pl.ds(start, 8)], s_u.at[i], r_u.at[i], anti)
        crossing.start()
        crossings.append(crossing)

    first = pl.ds(0, SPLIT)
    second = pl.ds(SPLIT, 80 - SPLIT)

    def phase_a(src, half):
        mine = eraw.at[c, half, y, x]
        for d in (1, 2, 3):
            remote(src.at[first], mine.at[first], s_a.at[half, 0], r_a.at[half, 0],
                   in_plane(y * 4 + (x + d) % 4, c)).start()
            remote(src.at[second], mine.at[second], s_a.at[half, 1], r_a.at[half, 1],
                   in_plane(((y + d) % 4) * 4 + x, c)).start()

    def phase_b(half):
        part = eraw.at[c, half]
        wait_for(part.at[0, pl.ds(0, 3), first], r_a.at[half, 0])
        row = part.at[y, :, first]
        for d in (1, 2, 3):
            remote(row, row, s_b.at[half, 0], r_b.at[half, 0], in_plane(((y + d) % 4) * 4 + x, c)).start()
        wait_for(part.at[0, pl.ds(0, 3), second], r_a.at[half, 1])
        column = part.at[:, x, second]
        for d in (1, 2, 3):
            remote(column, column, s_b.at[half, 1], r_b.at[half, 1], in_plane(y * 4 + (x + d) % 4, c)).start()

    def phase_d(half):
        part = eraw.at[c, half]
        wait_for(part.at[pl.ds(0, 3), :, first], r_b.at[half, 0])
        wait_for(part.at[pl.ds(0, 3), :, second], r_b.at[half, 1])
        remote(part, part, s_d.at[half], r_d.at[half], mate).start()

    def finish_e(half):
        part = eraw.at[c, half]
        wait_for(part.at[0, pl.ds(0, 3), first], s_a.at[half, 0])
        wait_for(part.at[0, pl.ds(0, 3), second], s_a.at[half, 1])
        wait_for(part.at[pl.ds(0, 3), :, first], s_b.at[half, 0])
        wait_for(part.at[pl.ds(0, 3), :, second], s_b.at[half, 1])
        wait_for(part, s_d.at[half])

    phase_a(chunk, 0)
    eraw[c, 0, y, x] = chunk[...]

    hub = 15 * h
    slot = yx * 2 + c

    def serve_row(src, half, shift):
        dest_y = (y + shift) % 4

        def serve(i, carry):
            dest = dest_y * 4 + (x + i // 2) % 4
            dest_c = (c + i % 2) % 2

            @pl.when((dest != hub) & (dest * 2 + dest_c != slot))
            def _():
                remote(src.at[pl.ds(dest * 2 + h, 2)], xraw.at[half, slot], s_x.at[half], r_x.at[half],
                       in_plane(dest, dest_c)).start()

            return carry

        lax.fori_loop(0, 8, serve, 0)

    def serve_hub(src, half):
        @pl.when(has_halo)
        def _():
            wait_for(vbuf.at[half], r_v.at[half])

        @pl.when(jnp.logical_not(has_halo))
        def _():
            vbuf[half] = jnp.zeros((16, TILE), BF)

        halo = vbuf[half]
        none = jnp.zeros_like(halo)
        ufix[half, 0] = src[31 * h] + jnp.where(h == 0, halo, none)
        ufix[half, 1] = src[31 * h + 1] + jnp.where(h == 1, halo, none)
        for dest_c in (0, 1):
            @pl.when(hub * 2 + dest_c != slot)
            def _():
                remote(ufix.at[half], xraw.at[half, slot], s_x.at[half], r_x.at[half],
                       in_plane(hub, dest_c)).start()

        @pl.when(yx == hub)
        def _():
            xraw[half, slot] = ufix[half]

        @pl.when(yx != hub)
        def _():
            xraw[half, slot] = src[pl.ds(yx * 2 + h, 2)]

    for shift in ORDER:
        serve_row(u, 0, shift)
    phase_b(0)
    serve_hub(u, 0)

    cross_e.wait_recv()
    phase_a(eraw.at[c, 1, y, x], 1)
    phase_d(0)
    for i, shift in enumerate(ORDER):
        crossings[i].wait_recv()
        serve_row(uin, 1, shift)
        if i == 1:
            phase_b(1)
    serve_hub(uin, 1)

    x_perm = perm(256, lambda o: ((o % 32) // 4) * 32 + (o // 32) * 4 + o % 4)
    e_perm = perm(256, lambda o: ((o % 8) // 4) * 128 + ((o % 64) // 8) * 16 + (o // 64) * 4 + o % 4)

    def ready_x(half):
        wait_for(xraw.at[half, pl.ds(0, 31)], r_x.at[half])
        for g in range(4):
            part = matmul(x_perm, xraw[half, pl.ds(g * 8, 8)].reshape(256, TILE)).astype(BF)
            for block in range(8):
                xw[half, block, pl.ds(g * 32, 32)] = part[block * 32:(block + 1) * 32]

    def ready_e(half):
        wait_for(eraw.at[1 - c, half], r_d.at[half])

        def group(kg, carry):
            rows = pl.ds(pl.multiple_of(kg * 16, 16), 16)
            for g in range(2):
                raw = eraw[:, half, pl.ds(g * 2, 2), :, rows]
                part = matmul(e_perm, raw.reshape(256, 256)).astype(BF)
                for k in range(4):
                    ew[half, kg * 4 + k, pl.ds(g * 64, 64)] = part[k * 64:(k + 1) * 64]
            return carry

        lax.fori_loop(0, 5, group, 0)

    def stage_one(half):
        for r in range(2):
            picked = [xw[half, jnp.clip(colidx[0, r, q] - first_col, 0, 7)] for q in range(3)]
            pair = jnp.concatenate(picked[:2], axis=1)

            def some(kg, carry):
                part = tv[pl.ds(kg * 4, 4), r]
                left = jnp.concatenate([part[:, 0], part[:, 1]], axis=2).reshape(512, 256)
                z = matmul_nt(left, pair) + matmul_nt(part[:, 2].reshape(512, TILE), picked[2])
                z = z.astype(BF)
                for k in range(4):
                    zbuf[kg * 2 + k // 2, pl.ds(r * TILE, TILE), pl.ds((k % 2) * TILE, TILE)] = z[k * TILE:(k + 1) * TILE]
                return carry

            lax.fori_loop(0, 5, some, 0)

    def stage_two(half):
        def pair_of(kk, total):
            return total + matmul(zbuf[kk], ew[half, pl.ds(kk * 2, 2)].reshape(256, 256))

        return lax.fori_loop(0, 10, pair_of, jnp.zeros((256, 256), F32))

    load.wait()
    ready_x(0)
    stage_one(0)
    phase_d(1)
    ready_e(0)
    acc[...] = stage_two(0)
    ready_e(1)
    ready_x(1)
    stage_one(1)
    total = (acc[...] + stage_two(1)).astype(BF)

    o_perm = perm(256, lambda o: ((o % 64) // 4) * 16 + ((o % 128) // 64) * 8 + (o // 128) * 4 + o % 4)
    ob[...] = matmul_nt(o_perm, total).astype(BF)
    swap = remote(ob.at[pl.ds(pl.multiple_of((1 - c) * 128, 128), 128)], oin, s_o, r_o, mate)
    swap.start()
    mine = ob[pl.ds(pl.multiple_of(c * 128, 128), 128)]
    f_perm = perm(256, lambda o: ((o % 16) // 4) * 64 + (o // 16) * 4 + o % 4)
    swap.wait_recv()
    theirs = oin[...]
    lower = jnp.where(c == 0, mine, theirs)
    upper = jnp.where(c == 0, theirs, mine)
    for dest_h in range(2):
        rows = slice(dest_h * 64, dest_h * 64 + 64)
        stack = jnp.concatenate([lower[rows, :TILE], lower[rows, TILE:], upper[rows, :TILE], upper[rows, TILE:]], axis=0)
        fb[dest_h] = matmul(f_perm, stack).astype(BF).reshape(16, 16, TILE)
    chip = yx * 2 + h

    def give_far(d, carry):
        other = (yx + d) % 16
        remote(fb.at[1 - h, other], out.at[chip], s_p, r_p, (other * 2 + 1 - h) * 2 + c).start()
        return carry

    def give_near(d, carry):
        other = (yx + d) % 16
        remote(fb.at[h, other], out.at[chip], s_p, r_p, (other * 2 + h) * 2 + c).start()
        return carry

    lax.fori_loop(0, 16, give_far, 0)
    lax.fori_loop(1, 16, give_near, 0)
    out[chip] = fb[h, yx]

    @pl.when(high)
    def _():
        send_right.wait_send()

    @pl.when(low)
    def _():
        send_left.wait_send()

    cross_e.wait_send()
    for crossing in crossings:
        crossing.wait_send()
    for half in (0, 1):
        finish_e(half)
        wait_for(xraw.at[half, pl.ds(0, 31)], s_x.at[half])
    swap.wait_send()
    wait_for(out.at[pl.ds(0, 31)], s_p)
    wait_for(out.at[pl.ds(0, 31)], r_p)


def shards(panels, tiles, coupling, pattern, colidx):
    cells = with_layout_constraint(panels.reshape(4, 128, TILE), Layout((1, 0, 2)))
    cells = jnp.transpose(cells, (1, 0, 2)).reshape(32, 16, TILE)
    values = with_layout_constraint(coupling.reshape(4, M, 2, TILE), Layout((1, 2, 0, 3)))
    values = jnp.transpose(values, (1, 2, 0, 3)).reshape(10, 16, TILE)
    blocks = jnp.transpose(pattern, (1, 2, 0))
    vmem = pl.BlockSpec(memory_space=pltpu.VMEM)
    dma = pltpu.SemaphoreType.DMA
    result = pl.pallas_call(
        kernel,
        name="galerkin",
        out_shape=jax.ShapeDtypeStruct((32, 16, TILE), BF),
        in_specs=[pl.BlockSpec(memory_space=pltpu.SMEM), vmem, vmem, vmem, pl.BlockSpec(memory_space=pl.ANY)],
        out_specs=vmem,
        scratch_shapes=[
            pltpu.VMEM((UNITS, 16, TILE), BF),
            pltpu.VMEM((80, 256), BF),
            pltpu.VMEM((M, 2, 3, TILE, TILE), BF),
            pltpu.VMEM((UNITS, 16, TILE), BF),
            pltpu.VMEM((2, 2, 16, TILE), BF),
            pltpu.VMEM((2, 16, TILE), BF),
            pltpu.VMEM((2, 32, 2, 16, TILE), BF),
            pltpu.VMEM((2, 8, TILE, TILE), BF),
            pltpu.VMEM((2, 2, 4, 4, 80, 256), BF),
            pltpu.VMEM((2, M, TILE, 256), BF),
            pltpu.VMEM((10, 256, 256), BF),
            pltpu.VMEM((256, 256), F32),
            pltpu.VMEM((256, 256), BF),
            pltpu.VMEM((TILE, 256), BF),
            pltpu.VMEM((2, 16, 16, TILE), BF),
            dma, dma((2,)), dma((2,)), dma, dma, dma((4,)), dma((4,)),
            dma((2, 2)), dma((2, 2)), dma((2, 2)), dma((2, 2)), dma((2,)), dma((2,)), dma((2,)), dma((2,)),
            dma, dma, dma, dma,
        ],
        compiler_params=pltpu.CompilerParams(collective_id=0, has_side_effects=True, vmem_limit_bytes=62 << 20),
        cost_estimate=pl.CostEstimate(flops=2_000_000_000, bytes_accessed=8_000_000, transcendentals=0),
    )(colidx, cells, values, blocks, tiles.reshape(M, 2, 3, TILE, TILE))
    result = jnp.transpose(result.reshape(128, 4, TILE), (1, 0, 2))
    return with_layout_constraint(result, Layout((1, 0, 2))).reshape(4, 128 * TILE)


def solution(mesh):
    in_specs = (
        P("chaos", "space"),
        P(None, "space", "chaos", None, None, None),
        P("chaos", None, None),
        P(),
        P("space", "chaos", None),
    )
    return jax.shard_map(shards, mesh=mesh, in_specs=in_specs, out_specs=P("chaos", "space"), check_vma=False)
```

```python
import jax
import jax.numpy as jnp
from jax import lax
from jax.experimental import pallas as pl
from jax.experimental.layout import Layout, with_layout_constraint
from jax.experimental.pallas import tpu as pltpu
from jax.sharding import PartitionSpec as P

M = 20
TILE = 128
CBLK = 64
BF = jnp.bfloat16
F32 = jnp.float32
UNITS = 33
SPLIT = 48
ORDER = (2, 1, 3, 0)


def perm(rows, source_of):
    out_row = lax.broadcasted_iota(jnp.int32, (rows, rows), 0)
    in_row = lax.broadcasted_iota(jnp.int32, (rows, rows), 1)
    return jnp.where(in_row == source_of(out_row), 1.0, 0.0).astype(BF)


def matmul(a, b):
    return lax.dot_general(a, b, (((1,), (0,)), ((), ())), preferred_element_type=F32)


def matmul_nt(a, b):
    return lax.dot_general(a, b, (((1,), (1,)), ((), ())), preferred_element_type=F32)


def kernel(colidx, cells_in, coupling_in, pattern_in, tiles, out,
           cells, coupling, pattern, ends, u, chunk, tv, uin, vbuf, xraw, xw, eraw, ew, zbuf, acc, ob, oin, fb,
           s_c, s_t, s_v, r_v, s_e, r_e, s_u, r_u, s_a, r_a, s_b, r_b, s_d, r_d, s_x, r_x, s_o, r_o, s_p, r_p):
    rank = lax.axis_index("chaos")
    s = lax.axis_index("space")
    c = rank % 2
    h = (rank // 2) % 2
    yx = rank // 4
    y = yx // 4
    x = yx % 4

    def remote(src, dst, send, recv, chaos, space=None):
        return pltpu.make_async_remote_copy(
            src_ref=src, dst_ref=dst, send_sem=send, recv_sem=recv,
            device_id={"chaos": chaos, "space": s if space is None else space},
            device_id_type=pl.DeviceIdType.MESH)

    def wait_for(ref, sem):
        pltpu.make_async_copy(ref, ref, sem).wait()

    def in_plane(dest_yx, dest_c):
        return (dest_yx * 2 + h) * 2 + dest_c

    anti = (yx * 2 + 1 - h) * 2 + c
    mate = (yx * 2 + h) * 2 + 1 - c
    low, high = s > 0, s < 7
    place = jnp.where(s < 4, s, 7 - s)
    at_border = place == 0
    border = jnp.where(s < 4, 7, 0)
    beyond = [jnp.where(s == 0, 7 - j, j) for j in range(4)]
    peers = [(s // 4) * 4 + (s + d) % 4 for d in (1, 2, 3)]
    flat = yx * 4 + c
    first_col = s * 128 + (rank // 2) * 4 - 2

    barrier = pltpu.get_barrier_semaphore()

    def greet(chaos, space):
        pl.semaphore_signal(barrier, inc=1, device_id={"chaos": chaos, "space": space},
                            device_id_type=pl.DeviceIdType.MESH)

    greet(anti, s)

    @pl.when(at_border)
    def _():
        for j in range(4):
            greet(anti, beyond[j])

    @pl.when(jnp.logical_not(at_border))
    def _():
        greet(anti, border)

    for peer in peers:
        greet(rank, peer)

    @pl.when(high)
    def _():
        greet(flat + 2 * h, s + 1)

    @pl.when(low)
    def _():
        greet(flat + 2 * h, s - 1)

    @pl.when(low & (h == 0))
    def _():
        greet(flat + 2, s - 1)

    @pl.when(high & (h == 1))
    def _():
        greet(flat, s + 1)

    def greet_plane(d, carry):
        other = (yx * 2 + c + d) % 32
        greet(in_plane(other // 2, other % 2), s)
        return carry

    lax.fori_loop(1, 32, greet_plane, 0, unroll=True)
    has_halo = (low & (h == 0)) | (high & (h == 1))

    fetches = []
    for i, (src, dst) in enumerate(((coupling_in, coupling), (pattern_in, pattern), (cells_in, cells))):
        fetches.append(pltpu.make_async_copy(src, dst, s_c.at[i]))
        fetches[-1].start()
    load = pltpu.make_async_copy(tiles, tv, s_t)
    load.start()

    row = lax.broadcasted_iota(jnp.int32, (80, M), 0)
    term = lax.broadcasted_iota(jnp.int32, (80, M), 1)
    spread = jnp.where(row // 4 == term, 1.0, 0.0).astype(BF)
    block = lax.broadcasted_iota(jnp.int32, (4, 256), 0)
    column = lax.broadcasted_iota(jnp.int32, (4, 256), 1)
    widen = jnp.where(column // CBLK == block, 1.0, 0.0).astype(BF)
    fetches[0].wait()
    fetches[1].wait()
    mask = matmul(matmul_nt(spread, pattern[y].astype(F32).astype(BF)).astype(BF), widen)
    out_row = lax.broadcasted_iota(jnp.int32, (80, 160), 0)
    in_row = lax.broadcasted_iota(jnp.int32, (80, 160), 1)
    raw = coupling[...].reshape(160, TILE)
    for part in range(2):
        take = jnp.where(in_row == (out_row // 4) * 8 + part * 4 + out_row % 4, 1.0, 0.0).astype(BF)
        lanes = slice(part * TILE, part * TILE + TILE)
        chunk[:, lanes] = (matmul(take, raw) * mask[:, lanes]).astype(BF)

    fetches[2].wait()
    gap = jnp.zeros((8, TILE), BF)
    u[...] = jnp.concatenate([gap, cells[...].reshape(512, TILE), gap], axis=0).reshape(UNITS, 16, TILE)
    ends[0] = u[0]
    ends[1] = u[UNITS - 1]
    pl.semaphore_wait(barrier, jnp.where(at_border, 39, 36) + low.astype(jnp.int32) + high.astype(jnp.int32) + has_halo.astype(jnp.int32))

    send_right = remote(ends.at[1], vbuf.at[h], s_v.at[0], r_v.at[h], flat, jnp.minimum(s + 1, 7))
    send_left = remote(ends.at[0], vbuf.at[1 - h], s_v.at[1], r_v.at[1 - h], flat + 2, jnp.maximum(s - 1, 0))

    @pl.when(high)
    def _():
        send_right.start()

    @pl.when(low)
    def _():
        send_left.start()

    crossings = []
    for i, shift in enumerate(ORDER):
        start = ((y + shift) % 4) * 8 + 1 - h
        crossing = remote(u.at[pl.ds(start, 8)], uin.at[pl.ds(start, 8)], s_u.at[i], r_u.at[i], anti)
        crossings.append(crossing)

    theirs_e = eraw.at[c, 1, y, x]

    def unit(j):
        return pl.ds(pl.multiple_of(j * 16, 16), 16)

    @pl.when(at_border)
    def _():
        for j in range(5):
            remote(chunk.at[unit(j)], theirs_e.at[unit(j)], s_e.at[0], r_e.at[0], anti, beyond[j % 4]).start()

    def exchange_e():
        def share(j):
            for peer in peers:
                remote(theirs_e.at[unit(j)], theirs_e.at[unit(j)], s_e.at[1], r_e.at[1], rank, peer).start()

        @pl.when(at_border)
        def _():
            wait_for(theirs_e.at[pl.ds(0, 32)], r_e.at[0])
            share(4)

        @pl.when(jnp.logical_not(at_border))
        def _():
            wait_for(theirs_e.at[pl.ds(0, 16)], r_e.at[0])

        share(place)

    def exchanged_e():
        @pl.when(at_border)
        def _():
            wait_for(theirs_e.at[pl.ds(0, 48)], r_e.at[1])

        @pl.when(jnp.logical_not(at_border))
        def _():
            wait_for(theirs_e.at[pl.ds(0, 64)], r_e.at[1])

    first = pl.ds(0, SPLIT)
    second = pl.ds(SPLIT, 80 - SPLIT)

    def phase_a(src, half):
        mine = eraw.at[c, half, y, x]
        for d in (1, 2, 3):
            remote(src.at[first], mine.at[first], s_a.at[half, 0], r_a.at[half, 0],
                   in_plane(y * 4 + (x + d) % 4, c)).start()
            remote(src.at[second], mine.at[second], s_a.at[half, 1], r_a.at[half, 1],
                   in_plane(((y + d) % 4) * 4 + x, c)).start()

    def phase_b(half):
        part = eraw.at[c, half]
        wait_for(part.at[0, pl.ds(0, 3), first], r_a.at[half, 0])
        row = part.at[y, :, first]
        for d in (1, 2, 3):
            remote(row, row, s_b.at[half, 0], r_b.at[half, 0], in_plane(((y + d) % 4) * 4 + x, c)).start()
        wait_for(part.at[0, pl.ds(0, 3), second], r_a.at[half, 1])
        column = part.at[:, x, second]
        for d in (1, 2, 3):
            remote(column, column, s_b.at[half, 1], r_b.at[half, 1], in_plane(y * 4 + (x + d) % 4, c)).start()

    def phase_d(half):
        part = eraw.at[c, half]
        wait_for(part.at[pl.ds(0, 3), :, first], r_b.at[half, 0])
        wait_for(part.at[pl.ds(0, 3), :, second], r_b.at[half, 1])
        remote(part, part, s_d.at[half], r_d.at[half], mate).start()

    def finish_e(half):
        part = eraw.at[c, half]
        wait_for(part.at[0, pl.ds(0, 3), first], s_a.at[half, 0])
        wait_for(part.at[0, pl.ds(0, 3), second], s_a.at[half, 1])
        wait_for(part.at[pl.ds(0, 3), :, first], s_b.at[half, 0])
        wait_for(part.at[pl.ds(0, 3), :, second], s_b.at[half, 1])
        wait_for(part, s_d.at[half])

    crossings[0].start()
    phase_a(chunk, 0)
    eraw[c, 0, y, x] = chunk[...]

    slot = yx * 2 + c

    def serve_row(src, half, dest_y, skip_own):
        for dx in range(4):
            for dc in range(2):
                if skip_own and dx == 0 and dc == 0:
                    continue
                dest = dest_y * 4 + (x + dx) % 4
                remote(src.at[pl.ds(dest * 2 + h, 2)], xraw.at[half, slot], s_x.at[half], r_x.at[half],
                       in_plane(dest, (c + dc) % 2)).start()
        if skip_own:
            xraw[half, slot] = src[pl.ds(yx * 2 + h, 2)]

    def merge_halo(src, half):
        @pl.when(has_halo)
        def _():
            wait_for(vbuf.at[half], r_v.at[half])
            src[32 * h] = src[32 * h] + vbuf[half]

    x_perm = perm(256, lambda o: ((o % 32) // 4) * 32 + (o // 32) * 4 + o % 4)
    e_perm = perm(256, lambda o: ((o % 8) // 4) * 128 + ((o % 64) // 8) * 16 + (o // 64) * 4 + o % 4)

    def ready_x(half):
        wait_for(xraw.at[half, pl.ds(0, 31)], r_x.at[half])
        for g in range(4):
            part = matmul(x_perm, xraw[half, pl.ds(g * 8, 8)].reshape(256, TILE)).astype(BF)
            for block in range(8):
                xw[half, block, pl.ds(g * 32, 32)] = part[block * 32:(block + 1) * 32]

    def ready_e(half):
        wait_for(eraw.at[1 - c, half], r_d.at[half])

        def group(kg, carry):
            rows = pl.ds(pl.multiple_of(kg * 16, 16), 16)
            for g in range(2):
                raw = eraw[:, half, pl.ds(g * 2, 2), :, rows]
                part = matmul(e_perm, raw.reshape(256, 256)).astype(BF)
                for k in range(4):
                    ew[half, kg * 4 + k, pl.ds(g * 64, 64)] = part[k * 64:(k + 1) * 64]
            return carry

        lax.fori_loop(0, 5, group, 0, unroll=True)

    def stage_one(half):
        for r in range(2):
            picked = [xw[half, jnp.clip(colidx[0, r, q] - first_col, 0, 7)] for q in range(3)]
            pair = jnp.concatenate(picked[:2], axis=1)

            def some(kg, carry):
                part = tv[pl.ds(kg * 4, 4), r]
                left = jnp.concatenate([part[:, 0], part[:, 1]], axis=2).reshape(512, 256)
                z = matmul_nt(left, pair) + matmul_nt(part[:, 2].reshape(512, TILE), picked[2])
                z = z.astype(BF)
                for k in range(4):
                    zbuf[kg * 2 + k // 2, pl.ds(r * TILE, TILE), pl.ds((k % 2) * TILE, TILE)] = z[k * TILE:(k + 1) * TILE]
                return carry

            lax.fori_loop(0, 5, some, 0, unroll=True)

    def stage_two(half):
        def pair_of(kk, total):
            return total + matmul(zbuf[kk], ew[half, pl.ds(kk * 2, 2)].reshape(256, 256))

        return lax.fori_loop(0, 10, pair_of, jnp.zeros((256, 256), F32), unroll=True)

    merge_halo(u, 0)
    exchange_e()
    for crossing in crossings[1:]:
        crossing.start()
    for shift in ORDER[:2]:
        serve_row(u, 0, (y + shift) % 4, shift == 0)
    phase_b(0)
    exchanged_e()
    phase_a(eraw.at[c, 1, y, x], 1)
    for shift in ORDER[2:]:
        serve_row(u, 0, (y + shift) % 4, shift == 0)
    phase_d(0)
    phase_b(1)
    for i, shift in enumerate(ORDER):
        dest_y = (y + shift) % 4
        crossings[i].wait_recv()

        @pl.when(dest_y == 3 * h)
        def _():
            merge_halo(uin, 1)

        serve_row(uin, 1, dest_y, shift == 0)
        if i == 0:
            load.wait()
            ready_x(0)
            ready_e(0)
        if i == 1:
            stage_one(0)
            phase_d(1)
        if i == 2:
            acc[...] = stage_two(0)
    ready_e(1)
    ready_x(1)
    stage_one(1)
    total = (acc[...] + stage_two(1)).astype(BF)

    o_perm = perm(256, lambda o: ((o % 64) // 4) * 16 + ((o % 128) // 64) * 8 + (o // 128) * 4 + o % 4)
    ob[...] = matmul_nt(o_perm, total).astype(BF)
    swap = remote(ob.at[pl.ds(pl.multiple_of((1 - c) * 128, 128), 128)], oin, s_o, r_o, mate)
    swap.start()
    mine = ob[pl.ds(pl.multiple_of(c * 128, 128), 128)]
    f_perm = perm(256, lambda o: ((o % 16) // 4) * 64 + (o // 16) * 4 + o % 4)
    swap.wait_recv()
    theirs = oin[...]
    lower = jnp.where(c == 0, mine, theirs)
    upper = jnp.where(c == 0, theirs, mine)
    for dest_h in range(2):
        rows = slice(dest_h * 64, dest_h * 64 + 64)
        stack = jnp.concatenate([lower[rows, :TILE], lower[rows, TILE:], upper[rows, :TILE], upper[rows, TILE:]], axis=0)
        fb[dest_h] = matmul(f_perm, stack).astype(BF).reshape(16, 16, TILE)
    chip = yx * 2 + h

    def give_far(d, carry):
        other = (yx + d) % 16
        remote(fb.at[1 - h, other], out.at[chip], s_p, r_p, (other * 2 + 1 - h) * 2 + c).start()
        return carry

    def give_near(d, carry):
        other = (yx + d) % 16
        remote(fb.at[h, other], out.at[chip], s_p, r_p, (other * 2 + h) * 2 + c).start()
        return carry

    lax.fori_loop(0, 16, give_far, 0, unroll=True)
    lax.fori_loop(1, 16, give_near, 0, unroll=True)
    out[chip] = fb[h, yx]

    @pl.when(high)
    def _():
        send_right.wait_send()

    @pl.when(low)
    def _():
        send_left.wait_send()


    @pl.when(at_border)
    def _():
        wait_for(chunk, s_e.at[0])
        wait_for(theirs_e.at[pl.ds(0, 48)], s_e.at[1])

    wait_for(theirs_e.at[pl.ds(0, 48)], s_e.at[1])
    for crossing in crossings:
        crossing.wait_send()
    for half in (0, 1):
        finish_e(half)
        wait_for(xraw.at[half, pl.ds(0, 31)], s_x.at[half])
    swap.wait_send()
    wait_for(out.at[pl.ds(0, 31)], s_p)
    wait_for(out.at[pl.ds(0, 31)], r_p)


def shards(panels, tiles, coupling, pattern, colidx):
    cells = with_layout_constraint(panels.reshape(4, 128, TILE), Layout((1, 0, 2)))
    cells = jnp.transpose(cells, (1, 0, 2)).reshape(32, 16, TILE)
    values = with_layout_constraint(coupling.reshape(4, M, 2, TILE), Layout((1, 2, 0, 3)))
    values = jnp.transpose(values, (1, 2, 0, 3)).reshape(10, 16, TILE)
    blocks = jnp.transpose(pattern, (1, 2, 0))
    vmem = pl.BlockSpec(memory_space=pltpu.VMEM)
    dma = pltpu.SemaphoreType.DMA
    result = pl.pallas_call(
        kernel,
        name="galerkin",
        out_shape=jax.ShapeDtypeStruct((32, 16, TILE), BF),
        in_specs=[pl.BlockSpec(memory_space=pltpu.SMEM)] + [pl.BlockSpec(memory_space=pltpu.HBM)] * 4,
        out_specs=vmem,
        scratch_shapes=[
            pltpu.VMEM((32, 16, TILE), BF),
            pltpu.VMEM((10, 16, TILE), BF),
            pltpu.VMEM((4, 4, M), jnp.int32),
            pltpu.VMEM((2, 16, TILE), BF),
            pltpu.VMEM((UNITS, 16, TILE), BF),
            pltpu.VMEM((80, 256), BF),
            pltpu.VMEM((M, 2, 3, TILE, TILE), BF),
            pltpu.VMEM((UNITS, 16, TILE), BF),
            pltpu.VMEM((2, 16, TILE), BF),
            pltpu.VMEM((2, 32, 2, 16, TILE), BF),
            pltpu.VMEM((2, 8, TILE, TILE), BF),
            pltpu.VMEM((2, 2, 4, 4, 80, 256), BF),
            pltpu.VMEM((2, M, TILE, 256), BF),
            pltpu.VMEM((10, 256, 256), BF),
            pltpu.VMEM((256, 256), F32),
            pltpu.VMEM((256, 256), BF),
            pltpu.VMEM((TILE, 256), BF),
            pltpu.VMEM((2, 16, 16, TILE), BF),
            dma((3,)), dma, dma((2,)), dma((2,)), dma((2,)), dma((2,)), dma((4,)), dma((4,)),
            dma((2, 2)), dma((2, 2)), dma((2, 2)), dma((2, 2)), dma((2,)), dma((2,)), dma((2,)), dma((2,)),
            dma, dma, dma, dma,
        ],
        compiler_params=pltpu.CompilerParams(collective_id=0, has_side_effects=True, vmem_limit_bytes=56 << 20),
        cost_estimate=pl.CostEstimate(flops=2_000_000_000, bytes_accessed=8_000_000, transcendentals=0),
    )(colidx, cells, values, blocks, tiles.reshape(M, 2, 3, TILE, TILE))
    result = jnp.transpose(result.reshape(128, 4, TILE), (1, 0, 2))
    return with_layout_constraint(result, Layout((1, 0, 2))).reshape(4, 128 * TILE)


def solution(mesh):
    in_specs = (
        P("chaos", "space"),
        P(None, "space", "chaos", None, None, None),
        P("chaos", None, None),
        P(),
        P("space", "chaos", None),
    )
    return jax.shard_map(shards, mesh=mesh, in_specs=in_specs, out_specs=P("chaos", "space"), check_vma=False)
```

```python
import jax
import jax.numpy as jnp
from jax import lax
from jax.experimental import pallas as pl
from jax.experimental.layout import Layout, with_layout_constraint
from jax.experimental.pallas import tpu as pltpu
from jax.sharding import PartitionSpec as P

M = 20
TILE = 128
CBLK = 64
BF = jnp.bfloat16
F32 = jnp.float32
UNITS = 33
SPLIT = 48
ORDER = (2, 1, 3, 0)


def perm(rows, source_of):
    out_row = lax.broadcasted_iota(jnp.int32, (rows, rows), 0)
    in_row = lax.broadcasted_iota(jnp.int32, (rows, rows), 1)
    return jnp.where(in_row == source_of(out_row), 1.0, 0.0).astype(BF)


def matmul(a, b):
    return lax.dot_general(a, b, (((1,), (0,)), ((), ())), preferred_element_type=F32)


def matmul_nt(a, b):
    return lax.dot_general(a, b, (((1,), (1,)), ((), ())), preferred_element_type=F32)


def kernel(colidx, cells_in, coupling_in, pattern_in, tiles, out,
           cells, coupling, pattern, ends, u, chunk, tv, uin, vbuf, xraw, xw, eraw, ew, zbuf, acc, ob, oin, fb,
           s_c, s_t, s_v, r_v, s_e, r_e, s_u, r_u, s_a, r_a, s_b, r_b, s_d, r_d, s_x, r_x, s_o, r_o, s_p, r_p):
    rank = lax.axis_index("chaos")
    s = lax.axis_index("space")
    c = rank % 2
    h = (rank // 2) % 2
    yx = rank // 4
    y = yx // 4
    x = yx % 4

    def remote(src, dst, send, recv, chaos, space=None):
        return pltpu.make_async_remote_copy(
            src_ref=src, dst_ref=dst, send_sem=send, recv_sem=recv,
            device_id={"chaos": chaos, "space": s if space is None else space},
            device_id_type=pl.DeviceIdType.MESH)

    def wait_for(ref, sem):
        pltpu.make_async_copy(ref, ref, sem).wait()

    def in_plane(dest_yx, dest_c):
        return (dest_yx * 2 + h) * 2 + dest_c

    anti = (yx * 2 + 1 - h) * 2 + c
    mate = (yx * 2 + h) * 2 + 1 - c
    low, high = s > 0, s < 7
    place = jnp.where(s < 4, s, 7 - s)
    at_border = place == 0
    border = jnp.where(s < 4, 7, 0)
    beyond = [jnp.where(s == 0, 7 - j, j) for j in range(4)]
    peers = [(s // 4) * 4 + (s + d) % 4 for d in (1, 2, 3)]
    flat = yx * 4 + c
    first_col = s * 128 + (rank // 2) * 4 - 2

    barrier = pltpu.get_barrier_semaphore()

    def greet(chaos, space):
        pl.semaphore_signal(barrier, inc=1, device_id={"chaos": chaos, "space": space},
                            device_id_type=pl.DeviceIdType.MESH)

    greet(anti, s)

    @pl.when(at_border)
    def _():
        for j in range(4):
            greet(anti, beyond[j])

    @pl.when(jnp.logical_not(at_border))
    def _():
        greet(anti, border)

    for peer in peers:
        greet(rank, peer)

    @pl.when(high)
    def _():
        greet(flat + 2 * h, s + 1)

    @pl.when(low)
    def _():
        greet(flat + 2 * h, s - 1)

    @pl.when(low & (h == 0))
    def _():
        greet(flat + 2, s - 1)

    @pl.when(high & (h == 1))
    def _():
        greet(flat, s + 1)

    def greet_plane(d, carry):
        other = (yx * 2 + c + d) % 32
        greet(in_plane(other // 2, other % 2), s)
        return carry

    lax.fori_loop(1, 32, greet_plane, 0, unroll=True)
    has_halo = (low & (h == 0)) | (high & (h == 1))

    fetches = []
    for i, (src, dst) in enumerate(((coupling_in, coupling), (pattern_in, pattern), (cells_in, cells))):
        fetches.append(pltpu.make_async_copy(src, dst, s_c.at[i]))
        fetches[-1].start()
    load = pltpu.make_async_copy(tiles, tv, s_t)
    load.start()

    row = lax.broadcasted_iota(jnp.int32, (80, M), 0)
    term = lax.broadcasted_iota(jnp.int32, (80, M), 1)
    spread = jnp.where(row // 4 == term, 1.0, 0.0).astype(BF)
    block = lax.broadcasted_iota(jnp.int32, (4, 256), 0)
    column = lax.broadcasted_iota(jnp.int32, (4, 256), 1)
    widen = jnp.where(column // CBLK == block, 1.0, 0.0).astype(BF)
    fetches[0].wait()
    fetches[1].wait()
    mask = matmul(matmul_nt(spread, pattern[y].astype(F32).astype(BF)).astype(BF), widen)
    out_row = lax.broadcasted_iota(jnp.int32, (80, 160), 0)
    in_row = lax.broadcasted_iota(jnp.int32, (80, 160), 1)
    raw = coupling[...].reshape(160, TILE)
    for part in range(2):
        take = jnp.where(in_row == (out_row // 4) * 8 + part * 4 + out_row % 4, 1.0, 0.0).astype(BF)
        lanes = slice(part * TILE, part * TILE + TILE)
        chunk[:, lanes] = (matmul(take, raw) * mask[:, lanes]).astype(BF)

    fetches[2].wait()
    gap = jnp.zeros((8, TILE), BF)
    u[...] = jnp.concatenate([gap, cells[...].reshape(512, TILE), gap], axis=0).reshape(UNITS, 16, TILE)
    ends[0] = u[0]
    ends[1] = u[UNITS - 1]
    pl.semaphore_wait(barrier, jnp.where(at_border, 39, 36) + low.astype(jnp.int32) + high.astype(jnp.int32) + has_halo.astype(jnp.int32))

    send_right = remote(ends.at[1], vbuf.at[h], s_v.at[0], r_v.at[h], flat, jnp.minimum(s + 1, 7))
    send_left = remote(ends.at[0], vbuf.at[1 - h], s_v.at[1], r_v.at[1 - h], flat + 2, jnp.maximum(s - 1, 0))

    @pl.when(high)
    def _():
        send_right.start()

    @pl.when(low)
    def _():
        send_left.start()

    crossings = []
    for i, shift in enumerate(ORDER):
        start = ((y + shift) % 4) * 8 + 1 - h
        crossing = remote(u.at[pl.ds(start, 8)], uin.at[pl.ds(start, 8)], s_u.at[i], r_u.at[i], anti)
        crossings.append(crossing)

    theirs_e = eraw.at[c, 1, y, x]

    def unit(j):
        return pl.ds(pl.multiple_of(j * 16, 16), 16)

    @pl.when(at_border)
    def _():
        for j in range(5):
            remote(chunk.at[unit(j)], theirs_e.at[unit(j)], s_e.at[0], r_e.at[0], anti, beyond[j % 4]).start()

    def exchange_e():
        def share(j):
            for peer in peers:
                remote(theirs_e.at[unit(j)], theirs_e.at[unit(j)], s_e.at[1], r_e.at[1], rank, peer).start()

        @pl.when(at_border)
        def _():
            wait_for(theirs_e.at[pl.ds(0, 32)], r_e.at[0])
            share(4)

        @pl.when(jnp.logical_not(at_border))
        def _():
            wait_for(theirs_e.at[pl.ds(0, 16)], r_e.at[0])

        share(place)

    def exchanged_e():
        @pl.when(at_border)
        def _():
            wait_for(theirs_e.at[pl.ds(0, 48)], r_e.at[1])

        @pl.when(jnp.logical_not(at_border))
        def _():
            wait_for(theirs_e.at[pl.ds(0, 64)], r_e.at[1])

    first = pl.ds(0, SPLIT)
    second = pl.ds(SPLIT, 80 - SPLIT)

    def phase_a(src, half):
        mine = eraw.at[c, half, y, x]
        for d in (1, 2, 3):
            remote(src.at[first], mine.at[first], s_a.at[half, 0], r_a.at[half, 0],
                   in_plane(y * 4 + (x + d) % 4, c)).start()
            remote(src.at[second], mine.at[second], s_a.at[half, 1], r_a.at[half, 1],
                   in_plane(((y + d) % 4) * 4 + x, c)).start()

    def phase_b(half):
        part = eraw.at[c, half]
        wait_for(part.at[0, pl.ds(0, 3), first], r_a.at[half, 0])
        row = part.at[y, :, first]
        for d in (1, 2, 3):
            remote(row, row, s_b.at[half, 0], r_b.at[half, 0], in_plane(((y + d) % 4) * 4 + x, c)).start()
        wait_for(part.at[0, pl.ds(0, 3), second], r_a.at[half, 1])
        column = part.at[:, x, second]
        for d in (1, 2, 3):
            remote(column, column, s_b.at[half, 1], r_b.at[half, 1], in_plane(y * 4 + (x + d) % 4, c)).start()

    def phase_d(half):
        part = eraw.at[c, half]
        wait_for(part.at[pl.ds(0, 3), :, first], r_b.at[half, 0])
        wait_for(part.at[pl.ds(0, 3), :, second], r_b.at[half, 1])
        remote(part, part, s_d.at[half], r_d.at[half], mate).start()

    def finish_e(half):
        part = eraw.at[c, half]
        wait_for(part.at[0, pl.ds(0, 3), first], s_a.at[half, 0])
        wait_for(part.at[0, pl.ds(0, 3), second], s_a.at[half, 1])
        wait_for(part.at[pl.ds(0, 3), :, first], s_b.at[half, 0])
        wait_for(part.at[pl.ds(0, 3), :, second], s_b.at[half, 1])
        wait_for(part, s_d.at[half])

    crossings[0].start()
    phase_a(chunk, 0)
    eraw[c, 0, y, x] = chunk[...]

    slot = yx * 2 + c

    def serve_row(src, half, dest_y, skip_own):
        for dx in range(4):
            for dc in range(2):
                if skip_own and dx == 0 and dc == 0:
                    continue
                dest = dest_y * 4 + (x + dx) % 4
                remote(src.at[pl.ds(dest * 2 + h, 2)], xraw.at[half, slot], s_x.at[half], r_x.at[half],
                       in_plane(dest, (c + dc) % 2)).start()
        if skip_own:
            xraw[half, slot] = src[pl.ds(yx * 2 + h, 2)]

    def merge_halo(src, half):
        @pl.when(has_halo)
        def _():
            wait_for(vbuf.at[half], r_v.at[half])
            src[32 * h] = src[32 * h] + vbuf[half]

    x_perm = perm(256, lambda o: ((o % 32) // 4) * 32 + (o // 32) * 4 + o % 4)
    e_perm = perm(256, lambda o: ((o % 8) // 4) * 128 + ((o % 64) // 8) * 16 + (o // 64) * 4 + o % 4)

    def ready_x(half):
        wait_for(xraw.at[half, pl.ds(0, 31)], r_x.at[half])
        for g in range(4):
            part = matmul(x_perm, xraw[half, pl.ds(g * 8, 8)].reshape(256, TILE)).astype(BF)
            for block in range(8):
                xw[half, block, pl.ds(g * 32, 32)] = part[block * 32:(block + 1) * 32]

    def ready_e(half):
        wait_for(eraw.at[1 - c, half], r_d.at[half])

        def group(kg, carry):
            rows = pl.ds(pl.multiple_of(kg * 16, 16), 16)
            for g in range(2):
                raw = eraw[:, half, pl.ds(g * 2, 2), :, rows]
                part = matmul(e_perm, raw.reshape(256, 256)).astype(BF)
                for k in range(4):
                    ew[half, kg * 4 + k, pl.ds(g * 64, 64)] = part[k * 64:(k + 1) * 64]
            return carry

        lax.fori_loop(0, 5, group, 0, unroll=True)

    def stage_one(half):
        for r in range(2):
            picked = [xw[half, jnp.clip(colidx[0, r, q] - first_col, 0, 7)] for q in range(3)]
            pair = jnp.concatenate(picked[:2], axis=1)

            def some(kg, carry):
                part = tv[pl.ds(kg * 4, 4), r]
                left = jnp.concatenate([part[:, 0], part[:, 1]], axis=2).reshape(512, 256)
                z = matmul_nt(left, pair) + matmul_nt(part[:, 2].reshape(512, TILE), picked[2])
                z = z.astype(BF)
                for k in range(4):
                    zbuf[kg * 2 + k // 2, pl.ds(r * TILE, TILE), pl.ds((k % 2) * TILE, TILE)] = z[k * TILE:(k + 1) * TILE]
                return carry

            lax.fori_loop(0, 5, some, 0, unroll=True)

    def stage_two(half):
        def pair_of(kk, total):
            return total + matmul(zbuf[kk], ew[half, pl.ds(kk * 2, 2)].reshape(256, 256))

        return lax.fori_loop(0, 10, pair_of, jnp.zeros((256, 256), F32), unroll=True)

    merge_halo(u, 0)
    exchange_e()
    for crossing in crossings[1:]:
        crossing.start()
    for shift in ORDER[:2]:
        serve_row(u, 0, (y + shift) % 4, shift == 0)
    phase_b(0)
    exchanged_e()
    phase_a(eraw.at[c, 1, y, x], 1)
    for shift in ORDER[2:]:
        serve_row(u, 0, (y + shift) % 4, shift == 0)
    for i, shift in enumerate(ORDER):
        dest_y = (y + shift) % 4
        crossings[i].wait_recv()

        @pl.when(dest_y == 3 * h)
        def _():
            merge_halo(uin, 1)

        serve_row(uin, 1, dest_y, shift == 0)
        if i == 0:
            phase_d(0)
            phase_b(1)
            load.wait()
            ready_x(0)
        if i == 1:
            stage_one(0)
            ready_e(0)
        if i == 2:
            acc[...] = stage_two(0)
    phase_d(1)
    ready_x(1)
    stage_one(1)
    ready_e(1)
    total = (acc[...] + stage_two(1)).astype(BF)

    o_perm = perm(256, lambda o: ((o % 64) // 4) * 16 + ((o % 128) // 64) * 8 + (o // 128) * 4 + o % 4)
    ob[...] = matmul_nt(o_perm, total).astype(BF)
    swap = remote(ob.at[pl.ds(pl.multiple_of((1 - c) * 128, 128), 128)], oin, s_o, r_o, mate)
    swap.start()
    mine = ob[pl.ds(pl.multiple_of(c * 128, 128), 128)]
    f_perm = perm(256, lambda o: ((o % 16) // 4) * 64 + (o // 16) * 4 + o % 4)
    swap.wait_recv()
    theirs = oin[...]
    lower = jnp.where(c == 0, mine, theirs)
    upper = jnp.where(c == 0, theirs, mine)
    for dest_h in range(2):
        rows = slice(dest_h * 64, dest_h * 64 + 64)
        stack = jnp.concatenate([lower[rows, :TILE], lower[rows, TILE:], upper[rows, :TILE], upper[rows, TILE:]], axis=0)
        fb[dest_h] = matmul(f_perm, stack).astype(BF).reshape(16, 16, TILE)
    chip = yx * 2 + h

    def give_far(d, carry):
        other = (yx + d) % 16
        remote(fb.at[1 - h, other], out.at[chip], s_p, r_p, (other * 2 + 1 - h) * 2 + c).start()
        return carry

    def give_near(d, carry):
        other = (yx + d) % 16
        remote(fb.at[h, other], out.at[chip], s_p, r_p, (other * 2 + h) * 2 + c).start()
        return carry

    lax.fori_loop(0, 16, give_far, 0, unroll=True)
    lax.fori_loop(1, 16, give_near, 0, unroll=True)
    out[chip] = fb[h, yx]

    @pl.when(high)
    def _():
        send_right.wait_send()

    @pl.when(low)
    def _():
        send_left.wait_send()


    @pl.when(at_border)
    def _():
        wait_for(chunk, s_e.at[0])
        wait_for(theirs_e.at[pl.ds(0, 48)], s_e.at[1])

    wait_for(theirs_e.at[pl.ds(0, 48)], s_e.at[1])
    for crossing in crossings:
        crossing.wait_send()
    for half in (0, 1):
        finish_e(half)
        wait_for(xraw.at[half, pl.ds(0, 31)], s_x.at[half])
    swap.wait_send()
    wait_for(out.at[pl.ds(0, 31)], s_p)
    wait_for(out.at[pl.ds(0, 31)], r_p)


def shards(panels, tiles, coupling, pattern, colidx):
    cells = with_layout_constraint(panels.reshape(4, 128, TILE), Layout((1, 0, 2)))
    cells = jnp.transpose(cells, (1, 0, 2)).reshape(32, 16, TILE)
    values = with_layout_constraint(coupling.reshape(4, M, 2, TILE), Layout((1, 2, 0, 3)))
    values = jnp.transpose(values, (1, 2, 0, 3)).reshape(10, 16, TILE)
    blocks = jnp.transpose(pattern, (1, 2, 0))
    vmem = pl.BlockSpec(memory_space=pltpu.VMEM)
    dma = pltpu.SemaphoreType.DMA
    result = pl.pallas_call(
        kernel,
        name="galerkin",
        out_shape=jax.ShapeDtypeStruct((32, 16, TILE), BF),
        in_specs=[pl.BlockSpec(memory_space=pltpu.SMEM)] + [pl.BlockSpec(memory_space=pltpu.HBM)] * 4,
        out_specs=vmem,
        scratch_shapes=[
            pltpu.VMEM((32, 16, TILE), BF),
            pltpu.VMEM((10, 16, TILE), BF),
            pltpu.VMEM((4, 4, M), jnp.int32),
            pltpu.VMEM((2, 16, TILE), BF),
            pltpu.VMEM((UNITS, 16, TILE), BF),
            pltpu.VMEM((80, 256), BF),
            pltpu.VMEM((M, 2, 3, TILE, TILE), BF),
            pltpu.VMEM((UNITS, 16, TILE), BF),
            pltpu.VMEM((2, 16, TILE), BF),
            pltpu.VMEM((2, 32, 2, 16, TILE), BF),
            pltpu.VMEM((2, 8, TILE, TILE), BF),
            pltpu.VMEM((2, 2, 4, 4, 80, 256), BF),
            pltpu.VMEM((2, M, TILE, 256), BF),
            pltpu.VMEM((10, 256, 256), BF),
            pltpu.VMEM((256, 256), F32),
            pltpu.VMEM((256, 256), BF),
            pltpu.VMEM((TILE, 256), BF),
            pltpu.VMEM((2, 16, 16, TILE), BF),
            dma((3,)), dma, dma((2,)), dma((2,)), dma((2,)), dma((2,)), dma((4,)), dma((4,)),
            dma((2, 2)), dma((2, 2)), dma((2, 2)), dma((2, 2)), dma((2,)), dma((2,)), dma((2,)), dma((2,)),
            dma, dma, dma, dma,
        ],
        compiler_params=pltpu.CompilerParams(collective_id=0, has_side_effects=True, vmem_limit_bytes=56 << 20),
        cost_estimate=pl.CostEstimate(flops=2_000_000_000, bytes_accessed=8_000_000, transcendentals=0),
    )(colidx, cells, values, blocks, tiles.reshape(M, 2, 3, TILE, TILE))
    result = jnp.transpose(result.reshape(128, 4, TILE), (1, 0, 2))
    return with_layout_constraint(result, Layout((1, 0, 2))).reshape(4, 128 * TILE)


def solution(mesh):
    in_specs = (
        P("chaos", "space"),
        P(None, "space", "chaos", None, None, None),
        P("chaos", None, None),
        P(),
        P("space", "chaos", None),
    )
    return jax.shard_map(shards, mesh=mesh, in_specs=in_specs, out_specs=P("chaos", "space"), check_vma=False)
```
